32 devices in a mesh: hyp: 4 (over y, x), row: 2 (over core), col: 4 (over z).
Axes of the slice: x: 2, y: 2, z: 4, core: 2. Of those that a mesh axis runs over, the one named last changes fastest.
Arguments:
- left_factors: bfloat16 [4, 48, 48, 256, 256], P('hyp', 'row', 'col'), may hold values from -0.0546875 to 0.0546875
- right_factors: bfloat16 [4, 48, 48, 256, 256], P('hyp', 'row', 'col'), may hold values from -0.375 to 0.375
- admissible: int32 [48, 48], P('row', 'col'), may hold values from 0 to 1, as said below
- tile_ranks: int32 [4, 48, 48], P('hyp', 'row', 'col'), may hold values from 32 to 256
- probes: bfloat16 [12288, 128], P('col', 'row'), may hold values from -6 to 6
- solved_probes: bfloat16 [12288, 128], P('row', 'col'), may hold values from -180 to 180
- data_terms: float32 [4], P('hyp'), may hold values from -64 to 64
- log_params: float32 [4], replicated, may hold values from -4 to 4
Outputs:
- forward: bfloat16 [4, 12288, 128], P('hyp', 'row', 'col')
- backward: bfloat16 [4, 12288, 128], P('hyp', 'col', 'row')
- new_params: float32 [4], replicated
The draws below stay inside these ranges and needn't reach their ends.
Inputs may be any that keep to these rules, and one draw needn't show every extreme that they name: `admissible`: Symmetric; diagonal tiles are near field (0); a tile is near field when it lies within a small drawn reach of the diagonal. `tile_ranks`: only read for far-field tiles.
All inputs are finite; a program needn't handle non-finite values.
Results may differ from the reference program's by a relative error of at most 0.0046.
The reference program's roundings to bfloat16 on the way count: a program that leaves them out, or rounds other values in their place, can miss the bound.
Values may be sent and summed in bfloat16 or wider, within the bound.
A program may use at most 128 MiB of HBM per device.

```python
import jax
import jax.numpy as jnp
from jax import lax

B = 256
R = 256
P_SIZE = 128
NB = 48
DERIVS = 4
N = 12288


def draw_admissible(key, part):
    reach = jax.random.randint(jax.random.fold_in(key, 11), (NB,), 0, 3)
    index = jnp.arange(NB).astype(jnp.int32)
    apart = jnp.abs(index[:, None] - index[None, :])
    near = apart <= jnp.maximum(reach[:, None], reach[None, :])
    return jnp.where(near, 0, 1).astype(jnp.int32)


def draw_solved_probes(key, part):
    first = jax.random.fold_in(jax.random.fold_in(key, 23), 0)
    rows = jnp.arange(NB * B).astype(jnp.float32) / (NB * B)
    cols = jnp.arange(P_SIZE).astype(jnp.float32) / P_SIZE
    base = jnp.clip(jax.random.normal(first, (NB * B, P_SIZE), jnp.float32), -6.0, 6.0)
    col_scale = jnp.power(3.0, cols)
    row_scale = jnp.power(10.0, rows)
    return (base * row_scale[:, None] * col_scale[None, :]).astype(jnp.bfloat16)


def plant(drawn, key, least, top_value):
    longest = drawn.shape.index(max(drawn.shape))
    spots = []
    for shift in (0, 1):
        where = [jax.random.randint(jax.random.fold_in(key, axis), (), 0, length) for axis, length in enumerate(drawn.shape)]
        where[longest] = (where[longest] + shift) % drawn.shape[longest]
        spots.append(tuple(where))
    return drawn.at[spots[0]].set(least).at[spots[1]].set(top_value)


def block_scale(own_key, shape, cuts, smallest, high):
    factor_of, own = 1.0, jax.random.fold_in(own_key, 6)
    for dim, blocks in cuts:
        heights = jnp.exp(jax.random.uniform(jax.random.fold_in(own, dim), (blocks,), jnp.float32, smallest / len(cuts), high / len(cuts)))
        factor_of = factor_of * jnp.repeat(heights, shape[dim] // blocks).reshape([-1 if axis == dim else 1 for axis in range(len(shape))])
    return factor_of


def bell_draw(key, extent, scale, limit, shards=(), kind=jnp.bfloat16):
    drawn = jax.random.normal(key, extent, jnp.float32) * scale
    if len(shards) > 0:
        drawn = block_scale(key, extent, shards, -0.22, 0.18) * drawn
    return jnp.clip(drawn, min=-limit, max=limit).astype(kind)


def setup_inputs(seed: int = 0) -> dict:
    seeds = jax.random.split(jax.random.key(seed), 9)
    return {
        "left_factors": bell_draw(seeds[0], (DERIVS, NB, NB, B, R), (R * NB) ** -0.5, 0.0546875, ((0, 4), (1, 2), (2, 4))),
        "right_factors": bell_draw(seeds[1], (DERIVS, NB, NB, B, R), B ** -0.5, 0.375, ((0, 4), (1, 2), (2, 4))),
        "admissible": draw_admissible(jax.random.fold_in(seeds[8], 71), 0),
        "tile_ranks": plant(jax.random.randint(seeds[3], (DERIVS, NB, NB), R // 8, R + 1), jax.random.fold_in(seeds[3], 1), R // 8, R).astype(jnp.int32),
        "probes": bell_draw(seeds[4], (N, P_SIZE), 1.0, 6.0, ((0, 4), (1, 2))),
        "solved_probes": draw_solved_probes(jax.random.fold_in(seeds[8], 71), 0),
        "data_terms": bell_draw(seeds[6], (DERIVS,), 10.0, 64.0, ((0, 4),), jnp.float32),
        "log_params": bell_draw(seeds[7], (DERIVS,), 1.0, 4.0, (), jnp.float32),
    }


step_rate = 0.5

def tile_masks(admissible, ranks):
    used = jnp.where(admissible == 0, R, ranks).astype(jnp.int32)
    slots = jnp.arange(R).astype(jnp.int32)
    return (slots[None, None, :] < used[:, :, None]).astype(jnp.float32)

def rounded(values):
    return lax.optimization_barrier(values.astype(jnp.bfloat16)).astype(jnp.float32)

def reference(left_factors, right_factors, admissible, tile_ranks, probes, solved_probes, data_terms, log_params):
    probe_blocks = probes.astype(jnp.float32).reshape(NB, B, P_SIZE)
    solved_blocks = solved_probes.astype(jnp.float32).reshape(NB, B, P_SIZE)
    solved_full = solved_probes.astype(jnp.float32)

    def one_matrix(items):
        left_tiles, right_tiles, ranks = items
        kept = tile_masks(admissible, ranks)

        def block_row(parts):
            left_row, right_row, kept_row = parts
            coefs = jnp.einsum('jbr,jbp->jrp', right_row.astype(jnp.float32), probe_blocks) * kept_row[:, :, None]
            return jnp.einsum('jbr,jrp->bp', left_row.astype(jnp.float32), rounded(coefs))

        def block_col(parts):
            left_col, right_col, kept_col = parts
            coefs = jnp.einsum('ibr,ibp->irp', left_col.astype(jnp.float32), solved_blocks) * kept_col[:, :, None]
            return jnp.einsum('ibr,irp->bp', right_col.astype(jnp.float32), rounded(coefs))
        rows_out = lax.map(block_row, (left_tiles, right_tiles, kept))
        cols_out = lax.map(block_col, (jnp.swapaxes(left_tiles, 0, 1), jnp.swapaxes(right_tiles, 0, 1), jnp.swapaxes(kept, 0, 1)))
        forward_full = rows_out.reshape(NB * B, P_SIZE)
        trace_value = jnp.sum(solved_full * forward_full) / P_SIZE
        return (forward_full.astype(jnp.bfloat16), cols_out.reshape(NB * B, P_SIZE).astype(jnp.bfloat16), trace_value)
    forward, backward, traces = lax.map(one_matrix, (left_factors, right_factors, tile_ranks))
    gradient = 0.5 * (data_terms - traces)
    grad_norm = jnp.sqrt(jnp.sum(gradient * gradient))
    new_params = log_params - step_rate * gradient / grad_norm
    return (forward, backward, new_params)
```

```python
import functools

import jax
import jax.numpy as jnp
from jax import lax
from jax.experimental import pallas as pl
from jax.experimental.pallas import tpu as pltpu
from jax.sharding import PartitionSpec as P

step_rate = 0.5
MESH = pl.DeviceIdType.MESH
F32 = jnp.float32
BF16 = jnp.bfloat16


def nn(a, b):
    return lax.dot_general(a, b, (((1,), (0,)), ((), ())), preferred_element_type=F32)


def nt(a, b):
    return lax.dot_general(a, b, (((1,), (1,)), ((), ())), preferred_element_type=F32)


def kernel(
    cfg,
    left_hbm,
    right_hbm,
    adm_ref,
    rank_ref,
    probe_ref,
    solved_ref,
    data_ref,
    logp_ref,
    fwd_ref,
    bwd_ref,
    newp_ref,
    left_buf,
    right_buf,
    probe_all,
    solved_all,
    part_f32,
    part_b16,
    fwd_in,
    back_acc,
    back_b16,
    back_in,
    tr_own,
    tr_row,
    tr_col,
    grad_all,
    tile_sem,
    p_sem,
    s1_sem,
    s2_sem,
    f_sem,
    b_sem,
    t_sem,
):
    nh, nr, nc, rows, cols, leaf, cap, lag, depth, slots = cfg
    hyp, row, col = lax.axis_index("hyp"), lax.axis_index("row"), lax.axis_index("col")
    probes = probe_all.shape[0]
    pr, pc = probe_ref.shape[0], solved_ref.shape[0]
    share = solved_ref.shape[1] // nh
    offset = (hyp * rows) // nh

    def row_of(t):
        return lax.rem(t + offset, rows)

    def peer(axis, me, n, d):
        return {axis: lax.rem(me + d, n)}

    def tile_copies(t):
        slot = lax.rem(t, slots)
        i = row_of(t)
        return (
            pltpu.make_async_copy(right_hbm.at[i], right_buf.at[slot], tile_sem.at[0, slot]),
            pltpu.make_async_copy(left_hbm.at[i], left_buf.at[slot], tile_sem.at[1, slot]),
        )

    def start_tiles(t):
        for c in tile_copies(t):
            c.start()

    for t in range(min(depth, rows)):
        start_tiles(t)

    barrier = pltpu.get_barrier_semaphore()
    for axis, me, n in (("row", row, nr), ("col", col, nc), ("hyp", hyp, nh)):
        for d in range(1, n):
            pl.semaphore_signal(barrier, inc=1, device_id=peer(axis, me, n, d), device_id_type=MESH)
    pl.semaphore_wait(barrier, nr + nc + nh - 3)

    def rows_p(r):
        return pl.ds(pl.multiple_of(r * pr, pr), pr)

    def rows_s(c):
        return pl.ds(pl.multiple_of(c * pc, pc), pc)

    def share_of(h):
        return pl.ds(pl.multiple_of(h * share, share), share)

    def remote(src, dst, sems, idx, device):
        return pltpu.make_async_remote_copy(
            src_ref=src,
            dst_ref=dst,
            send_sem=sems.at[(0,) + idx],
            recv_sem=sems.at[(1,) + idx],
            device_id=device,
            device_id_type=MESH,
        )

    p_copies = [
        remote(probe_ref, probe_all.at[rows_p(row)], p_sem, (d - 1,), peer("row", row, nr, d))
        for d in range(1, nr)
    ]
    for c in p_copies:
        c.start()
    s1_copies = [
        remote(
            solved_ref.at[:, share_of(hyp)],
            solved_all.at[rows_s(col), share_of(hyp)],
            s1_sem,
            (d - 1,),
            peer("col", col, nc, d),
        )
        for d in range(1, nc)
    ]
    for c in s1_copies:
        c.start()
    s2_copies = []
    for d in range(1, nc):
        src = solved_all.at[rows_s(lax.rem(col + nc - d, nc)), share_of(hyp)]
        for e in range(1, nh):
            s2_copies.append((d, remote(src, src, s2_sem, (d - 1, e - 1), peer("hyp", hyp, nh, e))))

    probe_all[rows_p(row), :] = probe_ref[...]
    solved_all[rows_s(col), :] = solved_ref[...]

    def zero(j, carry):
        back_acc[j] = jnp.zeros((probes, leaf), F32)
        return carry

    lax.fori_loop(0, cols, zero, 0)

    for c in p_copies:
        c.wait()

    lane = lax.broadcasted_iota(jnp.int32, (1, cap), 1)

    def keep(i, j, values):
        used = jnp.where(adm_ref[i, j] == 0, cap, rank_ref[i, j])
        return jnp.where(lane < used, values, 0.0).astype(BF16)

    def fwd_tile(slot, i, j, acc):
        coef = keep(i, j, nn(probe_all[:, j * leaf : (j + 1) * leaf], right_buf[slot, j]))
        return acc + nt(coef, left_buf[slot, j])

    def bwd_tile(slot, i, j, solved):
        coef = keep(i, j, nn(solved, left_buf[slot, j]))
        back_acc[j] += nt(coef, right_buf[slot, j])

    def send_part(i):
        return [
            remote(
                part_b16.at[i, rows_s(lax.rem(col + d, nc))],
                fwd_in.at[d - 1, i],
                f_sem,
                (d - 1,),
                peer("col", col, nc, d),
            )
            for d in range(1, nc)
        ]

    def step(t, fwd, bwd):
        if fwd:
            for c in tile_copies(t):
                c.wait()
            i, slot = row_of(t), lax.rem(t, slots)
            acc = jnp.zeros((probes, leaf), F32)
        if bwd:
            ib, slotb = row_of(t - lag), lax.rem(t - lag, slots)
            solved = solved_all[:, pl.ds(pl.multiple_of(ib * leaf, leaf), leaf)]
        for j in range(cols):
            if fwd:
                acc = fwd_tile(slot, i, j, acc)
            if bwd:
                bwd_tile(slotb, ib, j, solved)
        if fwd:
            part_f32[i] = acc
            part_b16[i] = acc.astype(BF16)
            for c in send_part(i):
                c.start()

    def run(lo, hi, fwd, bwd, fetch):
        def body(t, carry):
            step(t, fwd, bwd)
            if fetch:
                start_tiles(t + depth)
            return carry

        if hi > lo:
            lax.fori_loop(lo, hi, body, 0)

    early = max(lag - 2, 0)
    last_fetch = rows - depth
    run(0, min(early, last_fetch), True, False, True)
    run(min(early, last_fetch), early, True, False, False)
    for d in range(1, nc):
        s1_copies[d - 1].wait_recv()
        for dd, c in s2_copies:
            if dd == d:
                c.start()
    run(early, min(lag, last_fetch), True, False, True)
    run(max(early, min(lag, last_fetch)), lag, True, False, False)
    own = rows // nh if rows % nh == 0 else 0
    mid = min(lag + own, rows)
    run(lag, min(mid, last_fetch), True, True, True)
    run(max(lag, min(mid, last_fetch)), mid, True, True, False)
    for d, c in s2_copies:
        c.wait_recv()
    run(mid, max(mid, last_fetch), True, True, True)
    run(max(mid, last_fetch), rows, True, True, False)

    def trace_row(i, acc):
        s = solved_all[:, pl.ds(pl.multiple_of(i * leaf, leaf), leaf)].astype(F32)
        return acc + s * part_f32[i]

    def total(x):
        return jnp.full((8, 128), jnp.sum(x), F32)

    tr_own[0] = total(lax.fori_loop(0, rows, trace_row, jnp.zeros((probes, leaf), F32)))
    tr_copies = [
        [
            remote(tr_own.at[0], tr_row.at[d - 1], t_sem, (0, d - 1), peer("row", row, nr, d))
            for d in range(1, nr)
        ],
        [
            remote(tr_own.at[1], tr_col.at[d - 1], t_sem, (1, d - 1), peer("col", col, nc, d))
            for d in range(1, nc)
        ],
        [
            remote(tr_own.at[2], grad_all.at[d], t_sem, (2, d - 1), peer("hyp", hyp, nh, d))
            for d in range(1, nh)
        ],
    ]
    for c in tr_copies[0]:
        c.start()
    cut = [rows + lag * k // 4 for k in range(5)]
    run(cut[0], cut[1], False, True, False)
    for c in tr_copies[0]:
        c.wait()
    value = tr_own[0]
    for d in range(nr - 1):
        value = value + tr_row[d]
    tr_own[1] = value
    for c in tr_copies[1]:
        c.start()
    run(cut[1], cut[2], False, True, False)
    for c in tr_copies[1]:
        c.wait()
    value = tr_own[1]
    for d in range(nc - 1):
        value = value + tr_col[d]
    tr_own[2] = 0.5 * (data_ref[0] - value / probes)
    for c in tr_copies[2]:
        c.start()
    run(cut[2], cut[4], False, True, False)

    def narrow(j, carry):
        back_b16[j] = back_acc[j].astype(BF16)
        return carry

    lax.fori_loop(0, cols, narrow, 0)
    b_copies = [
        remote(
            back_b16.at[:, rows_p(lax.rem(row + d, nr))],
            back_in.at[d - 1],
            b_sem,
            (d - 1,),
            peer("row", row, nr, d),
        )
        for d in range(1, nr)
    ]
    for c in b_copies:
        c.start()

    for d in range(1, nc):
        whole = fwd_in.at[d - 1]
        pltpu.make_async_copy(whole, whole, f_sem.at[0, d - 1]).wait()
        pltpu.make_async_copy(whole, whole, f_sem.at[1, d - 1]).wait()

    def fwd_out(i, carry):
        value = part_f32[i, rows_s(col), :]
        for d in range(nc - 1):
            value = value + fwd_in[d, i].astype(F32)
        fwd_ref[:, pl.ds(pl.multiple_of(i * leaf, leaf), leaf)] = value.astype(BF16)
        return carry

    lax.fori_loop(0, rows, fwd_out, 0)

    for c in tr_copies[2]:
        c.wait()
    grads = [tr_own[2]] + [grad_all[d] for d in range(1, nh)]
    square = grads[0] * grads[0]
    for g in grads[1:]:
        square = square + g * g
    norm = jnp.sqrt(square)
    for d, g in enumerate(grads):
        j = lax.rem(hyp + nh - d, nh)
        newp_ref[j] = logp_ref[j] - (step_rate * g / norm)[0, 0]

    for c in b_copies:
        c.wait()
    for j in range(cols):
        value = back_acc[j, rows_p(row), :]
        for d in range(nr - 1):
            value = value + back_in[d, j].astype(F32)
        bwd_ref[:, j * leaf : (j + 1) * leaf] = value.astype(BF16)

    for c in s1_copies:
        c.wait_send()
    for _, c in s2_copies:
        c.wait_send()


def local(
    sizes,
    left_factors,
    right_factors,
    admissible,
    tile_ranks,
    probes,
    solved_probes,
    data_terms,
    log_params,
):
    nh, nr, nc = sizes
    left, right = left_factors[0], right_factors[0]
    rows, cols, leaf, cap = left.shape
    probe_t, solved_t = probes.T, solved_probes.T
    pr, pc = probe_t.shape[0], solved_t.shape[0]
    count = pr * nr
    row_bytes = 2 * cols * leaf * cap * left.dtype.itemsize
    depth = min(4, rows)
    lag = min(rows // 2, max(1, (44 << 20) // row_bytes - depth))
    slots = lag + depth
    cfg = (nh, nr, nc, rows, cols, leaf, cap, lag, depth, slots)
    vmem = pl.BlockSpec(memory_space=pltpu.VMEM)
    smem = pl.BlockSpec(memory_space=pltpu.SMEM)
    hbm = pl.BlockSpec(memory_space=pl.ANY)
    dma = pltpu.SemaphoreType.DMA
    fwd, bwd, newp = pl.pallas_call(
        functools.partial(kernel, cfg),
        out_shape=(
            jax.ShapeDtypeStruct((pc, rows * leaf), BF16),
            jax.ShapeDtypeStruct((pr, cols * leaf), BF16),
            jax.ShapeDtypeStruct((nh,), F32),
        ),
        in_specs=[hbm, hbm, smem, smem, vmem, vmem, smem, smem],
        out_specs=(vmem, vmem, smem),
        scratch_shapes=[
            pltpu.VMEM((slots, cols, leaf, cap), BF16),
            pltpu.VMEM((slots, cols, leaf, cap), BF16),
            pltpu.VMEM((count, cols * leaf), BF16),
            pltpu.VMEM((count, rows * leaf), BF16),
            pltpu.VMEM((rows, count, leaf), F32),
            pltpu.VMEM((rows, count, leaf), BF16),
            pltpu.VMEM((nc - 1, rows, pc, leaf), BF16),
            pltpu.VMEM((cols, count, leaf), F32),
            pltpu.VMEM((cols, count, leaf), BF16),
            pltpu.VMEM((nr - 1, cols, pr, leaf), BF16),
            pltpu.VMEM((3, 8, 128), F32),
            pltpu.VMEM((nr - 1, 8, 128), F32),
            pltpu.VMEM((nc - 1, 8, 128), F32),
            pltpu.VMEM((nh, 8, 128), F32),
            dma((2, slots)),
            dma((2, nr - 1)),
            dma((2, nc - 1)),
            dma((2, nc - 1, nh - 1)),
            dma((2, nc - 1)),
            dma((2, nr - 1)),
            dma((2, 3, max(nr, nc, nh) - 1)),
        ],
        compiler_params=pltpu.CompilerParams(
            collective_id=0, has_side_effects=True, vmem_limit_bytes=63 << 20
        ),
        cost_estimate=pl.CostEstimate(
            flops=8 * rows * cols * leaf * cap * count,
            bytes_accessed=rows * row_bytes,
            transcendentals=0,
        ),
    )(left, right, admissible, tile_ranks[0], probe_t, solved_t, data_terms, log_params)
    return fwd.T[None], bwd.T[None], newp


def solution(mesh):
    sizes = (mesh.shape["hyp"], mesh.shape["row"], mesh.shape["col"])
    return jax.shard_map(
        functools.partial(local, sizes),
        mesh=mesh,
        in_specs=(
            P("hyp", "row", "col", None, None),
            P("hyp", "row", "col", None, None),
            P("row", "col"),
            P("hyp", "row", "col"),
            P("col", "row"),
            P("row", "col"),
            P("hyp"),
            P(),
        ),
        out_specs=(P("hyp", "row", "col"), P("hyp", "col", "row"), P()),
        check_vma=False,
    )
```

```python
import functools

import jax
import jax.numpy as jnp
from jax import lax
from jax.experimental import pallas as pl
from jax.experimental.pallas import tpu as pltpu
from jax.sharding import PartitionSpec as P

step_rate = 0.5
MESH = pl.DeviceIdType.MESH
F32 = jnp.float32
BF16 = jnp.bfloat16


def nn(a, b):
    return lax.dot_general(a, b, (((1,), (0,)), ((), ())), preferred_element_type=F32)


def nt(a, b):
    return lax.dot_general(a, b, (((1,), (1,)), ((), ())), preferred_element_type=F32)


def kernel(
    cfg,
    left_hbm,
    right_hbm,
    adm_ref,
    rank_ref,
    probe_ref,
    solved_ref,
    data_ref,
    logp_ref,
    fwd_ref,
    bwd_ref,
    newp_ref,
    left_buf,
    right_buf,
    probe_all,
    solved_all,
    part_f32,
    part_b16,
    fwd_in,
    back_acc,
    back_b16,
    back_in,
    tr_own,
    tr_row,
    tr_col,
    grad_all,
    tile_sem,
    p_sem,
    s1_sem,
    s2_sem,
    f_sem,
    b_sem,
    t_sem,
):
    nh, nr, nc, rows, cols, leaf, cap, lag, depth, slots = cfg
    hyp, row, col = lax.axis_index("hyp"), lax.axis_index("row"), lax.axis_index("col")
    probes = probe_all.shape[0]
    pr, pc = probe_ref.shape[0], solved_ref.shape[0]
    share = solved_ref.shape[1] // nh
    offset = (hyp * rows) // nh

    def row_of(t):
        return lax.rem(t + offset, rows)

    def peer(axis, me, n, d):
        return {axis: lax.rem(me + d, n)}

    def tile_copies(t):
        slot = lax.rem(t, slots)
        i = row_of(t)
        return (
            pltpu.make_async_copy(right_hbm.at[i], right_buf.at[slot], tile_sem.at[0, slot]),
            pltpu.make_async_copy(left_hbm.at[i], left_buf.at[slot], tile_sem.at[1, slot]),
        )

    def start_tiles(t):
        for c in tile_copies(t):
            c.start()

    for t in range(min(depth, rows)):
        start_tiles(t)

    barrier = pltpu.get_barrier_semaphore()
    for axis, me, n in (("row", row, nr), ("col", col, nc), ("hyp", hyp, nh)):
        for d in range(1, n):
            pl.semaphore_signal(barrier, inc=1, device_id=peer(axis, me, n, d), device_id_type=MESH)
    pl.semaphore_wait(barrier, nr + nc + nh - 3)

    def rows_p(r):
        return pl.ds(pl.multiple_of(r * pr, pr), pr)

    def rows_s(c):
        return pl.ds(pl.multiple_of(c * pc, pc), pc)

    def share_of(h):
        return pl.ds(pl.multiple_of(h * share, share), share)

    def remote(src, dst, sems, idx, device):
        return pltpu.make_async_remote_copy(
            src_ref=src,
            dst_ref=dst,
            send_sem=sems.at[(0,) + idx],
            recv_sem=sems.at[(1,) + idx],
            device_id=device,
            device_id_type=MESH,
        )

    p_copies = [
        remote(probe_ref, probe_all.at[rows_p(row)], p_sem, (d - 1,), peer("row", row, nr, d))
        for d in range(1, nr)
    ]
    for c in p_copies:
        c.start()
    s1_copies = [
        remote(
            solved_ref.at[:, share_of(hyp)],
            solved_all.at[rows_s(col), share_of(hyp)],
            s1_sem,
            (d - 1,),
            peer("col", col, nc, d),
        )
        for d in range(1, nc)
    ]
    for c in s1_copies:
        c.start()
    s2_copies = []
    for d in range(1, nc):
        src = solved_all.at[rows_s(lax.rem(col + nc - d, nc)), share_of(hyp)]
        for e in range(1, nh):
            s2_copies.append((d, remote(src, src, s2_sem, (d - 1, e - 1), peer("hyp", hyp, nh, e))))

    probe_all[rows_p(row), :] = probe_ref[...]
    solved_all[rows_s(col), :] = solved_ref[...]

    def zero(j, carry):
        back_acc[j] = jnp.zeros((probes, leaf), F32)
        return carry

    lax.fori_loop(0, cols, zero, 0)

    for c in p_copies:
        c.wait()

    lane = lax.broadcasted_iota(jnp.int32, (1, cap), 1)

    def keep(i, j, values):
        used = jnp.where(adm_ref[i, j] == 0, cap, rank_ref[i, j])
        return jnp.where(lane < used, values, 0.0).astype(BF16)

    group = max(k for k in range(1, 5) if cols % k == 0)

    def send_part(i):
        return [
            remote(
                part_b16.at[i, rows_s(lax.rem(col + d, nc))],
                fwd_in.at[d - 1, i],
                f_sem,
                (d - 1,),
                peer("col", col, nc, d),
            )
            for d in range(1, nc)
        ]

    def step(t, fwd, bwd):
        if fwd:
            for c in tile_copies(t):
                c.wait()
            i, slot = row_of(t), lax.rem(t, slots)
            acc = jnp.zeros((probes, leaf), F32)
        if bwd:
            ib, slotb = row_of(t - lag), lax.rem(t - lag, slots)
            solved = solved_all[:, pl.ds(pl.multiple_of(ib * leaf, leaf), leaf)]
        held = None
        for g in range(0, cols + group, group):
            made = None
            if g < cols:
                made = ([], [])
                for j in range(g, g + group):
                    if fwd:
                        wide = nn(probe_all[:, j * leaf : (j + 1) * leaf], right_buf[slot, j])
                        made[0].append(keep(i, j, wide))
                    if bwd:
                        made[1].append(keep(ib, j, nn(solved, left_buf[slotb, j])))
            if held is not None:
                js = range(g - group, g)
                if fwd:
                    tiles = jnp.concatenate([left_buf[slot, j] for j in js], 1)
                    acc = acc + nt(jnp.concatenate(held[0], 1), tiles)
                if bwd:
                    for k, j in enumerate(js):
                        back_acc[j] += nt(held[1][k], right_buf[slotb, j])
            held = made
        if fwd:
            part_f32[i] = acc
            part_b16[i] = acc.astype(BF16)
            for c in send_part(i):
                c.start()

    def run(lo, hi, fwd, bwd, fetch):
        def body(t, carry):
            step(t, fwd, bwd)
            if fetch:
                start_tiles(t + depth)
            return carry

        if hi > lo:
            lax.fori_loop(lo, hi, body, 0)

    early = max(lag - 2, 0)
    last_fetch = rows - depth
    run(0, min(early, last_fetch), True, False, True)
    run(min(early, last_fetch), early, True, False, False)
    for d in range(1, nc):
        s1_copies[d - 1].wait_recv()
        for dd, c in s2_copies:
            if dd == d:
                c.start()
    run(early, min(lag, last_fetch), True, False, True)
    run(max(early, min(lag, last_fetch)), lag, True, False, False)
    own = rows // nh if rows % nh == 0 else 0
    mid = min(lag + own, rows)
    run(lag, min(mid, last_fetch), True, True, True)
    run(max(lag, min(mid, last_fetch)), mid, True, True, False)
    for d, c in s2_copies:
        c.wait_recv()
    run(mid, max(mid, last_fetch), True, True, True)
    run(max(mid, last_fetch), rows, True, True, False)

    def trace_row(i, acc):
        s = solved_all[:, pl.ds(pl.multiple_of(i * leaf, leaf), leaf)].astype(F32)
        return acc + s * part_f32[i]

    def total(x):
        return jnp.full((8, 128), jnp.sum(x), F32)

    tr_own[0] = total(lax.fori_loop(0, rows, trace_row, jnp.zeros((probes, leaf), F32)))
    tr_copies = [
        [
            remote(tr_own.at[0], tr_row.at[d - 1], t_sem, (0, d - 1), peer("row", row, nr, d))
            for d in range(1, nr)
        ],
        [
            remote(tr_own.at[1], tr_col.at[d - 1], t_sem, (1, d - 1), peer("col", col, nc, d))
            for d in range(1, nc)
        ],
        [
            remote(tr_own.at[2], grad_all.at[d], t_sem, (2, d - 1), peer("hyp", hyp, nh, d))
            for d in range(1, nh)
        ],
    ]
    for c in tr_copies[0]:
        c.start()
    cut = [rows + lag * k // 4 for k in range(5)]
    run(cut[0], cut[1], False, True, False)
    for c in tr_copies[0]:
        c.wait()
    value = tr_own[0]
    for d in range(nr - 1):
        value = value + tr_row[d]
    tr_own[1] = value
    for c in tr_copies[1]:
        c.start()
    run(cut[1], cut[2], False, True, False)
    for c in tr_copies[1]:
        c.wait()
    value = tr_own[1]
    for d in range(nc - 1):
        value = value + tr_col[d]
    tr_own[2] = 0.5 * (data_ref[0] - value / probes)
    for c in tr_copies[2]:
        c.start()
    run(cut[2], cut[4], False, True, False)

    def narrow(j, carry):
        back_b16[j] = back_acc[j].astype(BF16)
        return carry

    lax.fori_loop(0, cols, narrow, 0)
    b_copies = [
        remote(
            back_b16.at[:, rows_p(lax.rem(row + d, nr))],
            back_in.at[d - 1],
            b_sem,
            (d - 1,),
            peer("row", row, nr, d),
        )
        for d in range(1, nr)
    ]
    for c in b_copies:
        c.start()

    for d in range(1, nc):
        whole = fwd_in.at[d - 1]
        pltpu.make_async_copy(whole, whole, f_sem.at[0, d - 1]).wait()
        pltpu.make_async_copy(whole, whole, f_sem.at[1, d - 1]).wait()

    def fwd_out(i, carry):
        value = part_f32[i, rows_s(col), :]
        for d in range(nc - 1):
            value = value + fwd_in[d, i].astype(F32)
        fwd_ref[:, pl.ds(pl.multiple_of(i * leaf, leaf), leaf)] = value.astype(BF16)
        return carry

    lax.fori_loop(0, rows, fwd_out, 0)

    for c in tr_copies[2]:
        c.wait()
    grads = [tr_own[2]] + [grad_all[d] for d in range(1, nh)]
    square = grads[0] * grads[0]
    for g in grads[1:]:
        square = square + g * g
    norm = jnp.sqrt(square)
    for d, g in enumerate(grads):
        j = lax.rem(hyp + nh - d, nh)
        newp_ref[j] = logp_ref[j] - (step_rate * g / norm)[0, 0]

    for c in b_copies:
        c.wait()
    for j in range(cols):
        value = back_acc[j, rows_p(row), :]
        for d in range(nr - 1):
            value = value + back_in[d, j].astype(F32)
        bwd_ref[:, j * leaf : (j + 1) * leaf] = value.astype(BF16)

    for c in s1_copies:
        c.wait_send()
    for _, c in s2_copies:
        c.wait_send()


def local(
    sizes,
    left_factors,
    right_factors,
    admissible,
    tile_ranks,
    probes,
    solved_probes,
    data_terms,
    log_params,
):
    nh, nr, nc = sizes
    left, right = left_factors[0], right_factors[0]
    rows, cols, leaf, cap = left.shape
    probe_t, solved_t = probes.T, solved_probes.T
    pr, pc = probe_t.shape[0], solved_t.shape[0]
    count = pr * nr
    row_bytes = 2 * cols * leaf * cap * left.dtype.itemsize
    depth = min(4, rows)
    lag = min(rows // 2, max(1, (44 << 20) // row_bytes - depth))
    slots = lag + depth
    cfg = (nh, nr, nc, rows, cols, leaf, cap, lag, depth, slots)
    vmem = pl.BlockSpec(memory_space=pltpu.VMEM)
    smem = pl.BlockSpec(memory_space=pltpu.SMEM)
    hbm = pl.BlockSpec(memory_space=pl.ANY)
    dma = pltpu.SemaphoreType.DMA
    fwd, bwd, newp = pl.pallas_call(
        functools.partial(kernel, cfg),
        out_shape=(
            jax.ShapeDtypeStruct((pc, rows * leaf), BF16),
            jax.ShapeDtypeStruct((pr, cols * leaf), BF16),
            jax.ShapeDtypeStruct((nh,), F32),
        ),
        in_specs=[hbm, hbm, smem, smem, vmem, vmem, smem, smem],
        out_specs=(vmem, vmem, smem),
        scratch_shapes=[
            pltpu.VMEM((slots, cols, leaf, cap), BF16),
            pltpu.VMEM((slots, cols, leaf, cap), BF16),
            pltpu.VMEM((count, cols * leaf), BF16),
            pltpu.VMEM((count, rows * leaf), BF16),
            pltpu.VMEM((rows, count, leaf), F32),
            pltpu.VMEM((rows, count, leaf), BF16),
            pltpu.VMEM((nc - 1, rows, pc, leaf), BF16),
            pltpu.VMEM((cols, count, leaf), F32),
            pltpu.VMEM((cols, count, leaf), BF16),
            pltpu.VMEM((nr - 1, cols, pr, leaf), BF16),
            pltpu.VMEM((3, 8, 128), F32),
            pltpu.VMEM((nr - 1, 8, 128), F32),
            pltpu.VMEM((nc - 1, 8, 128), F32),
            pltpu.VMEM((nh, 8, 128), F32),
            dma((2, slots)),
            dma((2, nr - 1)),
            dma((2, nc - 1)),
            dma((2, nc - 1, nh - 1)),
            dma((2, nc - 1)),
            dma((2, nr - 1)),
            dma((2, 3, max(nr, nc, nh) - 1)),
        ],
        compiler_params=pltpu.CompilerParams(
            collective_id=0, has_side_effects=True, vmem_limit_bytes=63 << 20
        ),
        cost_estimate=pl.CostEstimate(
            flops=8 * rows * cols * leaf * cap * count,
            bytes_accessed=rows * row_bytes,
            transcendentals=0,
        ),
    )(left, right, admissible, tile_ranks[0], probe_t, solved_t, data_terms, log_params)
    return fwd.T[None], bwd.T[None], newp


def solution(mesh):
    sizes = (mesh.shape["hyp"], mesh.shape["row"], mesh.shape["col"])
    return jax.shard_map(
        functools.partial(local, sizes),
        mesh=mesh,
        in_specs=(
            P("hyp", "row", "col", None, None),
            P("hyp", "row", "col", None, None),
            P("row", "col"),
            P("hyp", "row", "col"),
            P("col", "row"),
            P("row", "col"),
            P("hyp"),
            P(),
        ),
        out_specs=(P("hyp", "row", "col"), P("hyp", "col", "row"), P()),
        check_vma=False,
    )
```
